128 devices in a mesh: rep: 64 (over z, y, x), shard: 2 (over core).
Axes of the slice: x: 4, y: 4, z: 4, core: 2. Of those that a mesh axis runs over, the one named last changes fastest.
Arguments:
- hidden_in: bfloat16 [16384, 896], P(('rep', 'shard')), may hold values from -6 to 6
- seq_lengths: int32 [64, 2], P('rep'), may hold values from 32 to 224, as said below
- block_owner: int32 [64, 2], P('rep'), may hold values from 0 to 1, each once within a row
- norm_attn: bfloat16 [2, 896], P(None, 'shard'), may hold values from 0.099609375 to 1.8984375
- w_qkv: bfloat16 [2, 896, 1152], P(None, 'shard'), may hold values from -0.1875 to 0.1875
- b_qkv: bfloat16 [2, 1152], P(None, 'shard'), may hold values from -3 to 3
- w_out: bfloat16 [2, 896, 896], P(None, 'shard'), may hold values from -0.75 to 0.75
- norm_mlp: bfloat16 [2, 896], P(None, 'shard'), may hold values from 0.099609375 to 1.8984375
- w_gate_up: bfloat16 [2, 896, 9728], P(None, 'shard'), may hold values from -0.1875 to 0.1875
- w_down: bfloat16 [2, 4864, 896], P(None, 'shard'), may hold values from -0.125 to 0.125
- grad_out: float32 [16384, 896], P(('rep', 'shard')), may hold values from -6 to 6
Outputs:
- hidden_out: bfloat16 [16384, 896], P(('rep', 'shard'))
- grad_in: float32 [16384, 896], P(('rep', 'shard'))
- grad_norm_attn: float32 [2, 896], P(None, 'shard')
- grad_w_qkv: float32 [2, 896, 1152], P(None, 'shard')
- grad_b_qkv: float32 [2, 1152], P(None, 'shard')
- grad_w_out: float32 [2, 896, 896], P(None, 'shard')
- grad_norm_mlp: float32 [2, 896], P(None, 'shard')
- grad_w_gate_up: float32 [2, 896, 9728], P(None, 'shard')
- grad_w_down: float32 [2, 4864, 896], P(None, 'shard')
The draws below stay inside these ranges and needn't reach their ends.
Inputs may be any that keep to these rules, and one draw needn't show every extreme that they name: `seq_lengths`: each row lists the lengths of the 2 documents of one group's stream in stream order; they sum to 256; one of them is exactly 224, which one is drawn from the seed. `block_owner`: each row is a permutation: device s of group g holds stream positions block_owner[g, s] * 128 onwards, 128 of them.
All inputs are finite; a program needn't handle non-finite values.
Results may differ from the reference program's by a relative error of at most 0.015.
Values may be sent and summed in bfloat16 or wider, within the bound.
No kernel may reach another device: no remote copies, remote signals or barrier semaphores. Data moves between devices by JAX's collectives and lax.ppermute only.
A program may use at most 384 MiB of HBM per device.

```python
import jax
import jax.numpy as jnp
from jax import lax

D = 896
HEADS = 14
KV_HEADS = 2
HEAD = 64
FF = 4864
LAYERS = 2
TOK_DEV = 128
GROUP_TOK = 256
TOKENS = 16384
LONGEST = 224
GROUPS = 64
BLOCKS = 2
QKV = 1152
N_REP = 64
N_SHARD = 2


def draw_seq_lengths(key, part):
    key = jax.random.fold_in(key, 11)
    flipped = jax.random.randint(key, (GROUPS,), 0, 2).astype(jnp.int32)
    first_len = jnp.where(flipped == 1, LONGEST, GROUP_TOK - LONGEST).astype(jnp.int32)
    return jnp.stack([first_len, GROUP_TOK - first_len], axis=1).astype(jnp.int32)


def levels(key, extent, cuts, smallest, largest):
    factor_of = 1.0
    for axis_at, blocks in cuts:
        draws = jax.random.uniform(jax.random.fold_in(jax.random.fold_in(key, 6), axis_at), (blocks,), jnp.float32, smallest / len(cuts), largest / len(cuts))
        factor_of = factor_of * jnp.repeat(jnp.exp(draws), extent[axis_at] // blocks).reshape((-1,) + (1,) * (len(extent) - 1 - axis_at))
    return factor_of


def bell_draw(stream_key, dims, scale, bound, split=(), kind=jnp.bfloat16):
    array = scale * jax.random.normal(stream_key, dims, jnp.float32)
    if split:
        array = array * levels(stream_key, dims, split, -0.22, 0.18)
    return jnp.clip(array, -bound, bound).astype(kind)


def setup_inputs(seed: int = 0) -> dict:
    keys = jax.random.split(jax.random.key(seed), 12)
    return {
        "hidden_in": bell_draw(keys[0], (TOKENS, D), 1.0, 6.0, ((0, 128),)),
        "seq_lengths": draw_seq_lengths(jax.random.fold_in(keys[11], 71), 0),
        "block_owner": jax.vmap(lambda own: jax.random.permutation(own, BLOCKS))(jax.random.split(keys[2], GROUPS)).reshape((GROUPS, BLOCKS)).astype(jnp.int32),
        "norm_attn": jnp.clip(1.0 + 0.18 * jax.random.normal(keys[3], (LAYERS, D), jnp.float32), 0.099609375, 1.8984375).astype(jnp.bfloat16),
        "w_qkv": bell_draw(keys[4], (LAYERS, D, QKV), D ** -0.5, 0.1875, ((1, 2),)),
        "b_qkv": bell_draw(keys[5], (LAYERS, QKV), 0.5, 3.0, ((1, 2),)),
        "w_out": bell_draw(keys[6], (LAYERS, HEADS * HEAD, D), (HEADS * HEAD // 16) ** -0.5, 0.75, ((1, 2),)),
        "norm_mlp": jnp.clip(1.0 + 0.18 * jax.random.normal(keys[7], (LAYERS, D), jnp.float32), 0.099609375, 1.8984375).astype(jnp.bfloat16),
        "w_gate_up": bell_draw(keys[8], (LAYERS, D, 2 * FF), D ** -0.5, 0.1875, ((1, 2),)),
        "w_down": bell_draw(keys[9], (LAYERS, FF, D), (FF // 2) ** -0.5, 0.125, ((1, 2),)),
        "grad_out": bell_draw(keys[10], (TOKENS, D), 1.0, 6.0, ((0, 128),), jnp.float32),
    }


@jax.custom_vjp
def low(v):
    return lax.optimization_barrier(v.astype(jnp.bfloat16)).astype(jnp.float32)

@jax.custom_vjp
def low_back(v):
    return v

def low_keep(v):
    return (low(v), None)

def low_pass(kept, grad):
    return (grad,)

def back_keep(v):
    return (v, None)

def back_low(kept, grad):
    return (low(grad),)
low.defvjp(low_keep, low_pass)
low_back.defvjp(back_keep, back_low)
epsilon = 1e-06
base_freq = 1000000.0
highest = lax.Precision.HIGHEST

def rms_scale(values, gain_row):
    return values * lax.rsqrt(lax.optimization_barrier(jnp.mean(values * values, axis=1, keepdims=True)) + epsilon) * gain_row

def rotate(values, cosine, sine_part):
    half_width = values.shape[-1] // 2
    first_half = values[..., :half_width]
    second = values[..., half_width:]
    return jnp.concatenate([first_half * cosine - second * sine_part, second * cosine + first_half * sine_part], axis=-1)

def doc_position(stream, lengths):
    doc_ends = jnp.cumsum(lengths).astype(jnp.int32)
    doc_ids = lax.optimization_barrier(jnp.sum((stream[:, None] >= doc_ends[None, :]).astype(jnp.int32), axis=1))
    starts = lax.optimization_barrier(jnp.max(jnp.where(doc_ends[None, :] <= stream[:, None], doc_ends[None, :], 0), axis=1))
    return (doc_ids, (stream - starts).astype(jnp.int32))

def angles(positions, head_size):
    half_width = head_size // 2
    frequency = jnp.power(base_freq, -(jnp.arange(half_width, dtype=jnp.float32) * 2.0 / head_size))
    turned = positions.astype(jnp.float32)[:, None] * frequency[None, :]
    return (jnp.cos(turned)[:, None, :], jnp.sin(turned)[:, None, :])

def block_forward(residual, weights, cosine, sine_part, allowed):
    gain_attn, w_proj, b_proj, w_attn_out, gain_mlp, w_gu, w_dn = weights
    width_q = HEADS * HEAD
    width_k = KV_HEADS * HEAD
    per_group = HEADS // KV_HEADS
    normed = low(rms_scale(residual, gain_attn))
    projected = low_back(jnp.dot(normed, w_proj, precision=highest) + b_proj)
    queries = projected[:, :width_q].reshape(-1, HEADS, HEAD)
    rot_keys = projected[:, width_q:width_q + width_k].reshape(-1, KV_HEADS, HEAD)
    values = low(projected[:, width_q + width_k:].reshape(-1, KV_HEADS, HEAD))
    queries = low(rotate(queries, cosine, sine_part)).reshape(-1, KV_HEADS, per_group, HEAD)
    rot_keys = low(rotate(rot_keys, cosine, sine_part))
    scores = low_back(jnp.einsum('qcgd,kcd->cgqk', queries, rot_keys, precision=highest) * HEAD ** (-0.5))
    scores = jnp.where(allowed, scores, -1e+30)
    attn_probs = jax.nn.softmax(scores, axis=-1)
    attn_mixed = jnp.einsum('cgqk,kcd->qcgd', low(attn_probs), values, precision=highest).reshape(-1, width_q)
    attn_mixed = low_back(low(attn_mixed))
    middle = residual + low_back(jnp.dot(attn_mixed, w_attn_out, precision=highest))
    normed_mlp = low(rms_scale(middle, gain_mlp))
    gate_up = low_back(jnp.dot(normed_mlp, w_gu, precision=highest))
    hidden = low(jax.nn.silu(gate_up[:, :FF]) * gate_up[:, FF:])
    return middle + low_back(jnp.dot(hidden, w_dn, precision=highest))

def reference(hidden_in, seq_lengths, block_owner, norm_attn, w_qkv, b_qkv, w_out, norm_mlp, w_gate_up, w_down, grad_out):
    weights = tuple((member.astype(jnp.float32) for member in (norm_attn, w_qkv, b_qkv, w_out, norm_mlp, w_gate_up, w_down)))
    group_tok = TOK_DEV * N_SHARD
    inputs = hidden_in.astype(jnp.float32).reshape(N_REP, group_tok, D)
    cotangents = grad_out.astype(jnp.float32).reshape(N_REP, group_tok, D)
    offsets = jnp.arange(TOK_DEV, dtype=jnp.int32)

    def one_group(totals, member):
        residual, cotangent, lengths, owner_row = member
        stream = (owner_row.astype(jnp.int32)[:, None] * TOK_DEV + offsets[None, :]).reshape(-1).astype(jnp.int32)
        doc_ids, positions = doc_position(stream, lengths.astype(jnp.int32))
        allowed = (doc_ids[:, None] == doc_ids[None, :]) & (stream[None, :] <= stream[:, None])
        cosine, sine_part = angles(positions, HEAD)

        def forward(current, params):
            for depth_index in range(LAYERS):
                current = block_forward(current, tuple((param[depth_index] for param in params)), cosine, sine_part, allowed)
            return current
        result, pull_back = jax.vjp(forward, residual, weights)
        grad_resid, grad_weights = pull_back(cotangent)
        totals = tuple((running + added for running, added in zip(totals, grad_weights)))
        return (totals, (result.astype(jnp.bfloat16), grad_resid))
    start_totals = tuple((jnp.zeros_like(param) for param in weights))
    totals, (results, grads) = lax.scan(one_group, start_totals, (inputs, cotangents, seq_lengths, block_owner))
    return (results.reshape(N_REP * group_tok, D), grads.reshape(N_REP * group_tok, D), totals[0], totals[1], totals[2], totals[3], totals[4], totals[5], totals[6])
```

```python
import functools

import jax
import jax.numpy as jnp
from jax import lax
from jax.experimental import pallas as pl
from jax.experimental.pallas import tpu as pltpu
from jax.sharding import PartitionSpec as P

HEADS = 14
KV_HEADS = 2
HEAD = 64
D = 896
HALF = 448
FF = 4864
FH = 2432
QKV = 1152
TOK = 128

epsilon = 1e-06
base_freq = 1000000.0
VMEM = 60 * 1024 * 1024
F32 = jnp.float32
BF = jnp.bfloat16


def rms_scale(values, gain_row):
    return values * lax.rsqrt(jnp.mean(values * values, axis=1, keepdims=True) + epsilon) * gain_row


def rotate(values, cosine, sine_part):
    half_width = values.shape[-1] // 2
    first_half = values[..., :half_width]
    second = values[..., half_width:]
    return jnp.concatenate(
        [first_half * cosine - second * sine_part, second * cosine + first_half * sine_part],
        axis=-1,
    )


def doc_position(stream, lengths):
    doc_ends = jnp.cumsum(lengths)
    doc_ids = jnp.sum((stream[:, None] >= doc_ends[None, :]).astype(jnp.int32), axis=1)
    starts = jnp.max(jnp.where(doc_ends[None, :] <= stream[:, None], doc_ends[None, :], 0), axis=1)
    return (doc_ids, stream - starts)


def angles(positions, head_size):
    half_width = head_size // 2
    frequency = jnp.power(base_freq, -(jnp.arange(half_width, dtype=F32) * 2.0 / head_size))
    turned = positions.astype(F32)[:, None] * frequency[None, :]
    return (jnp.cos(turned)[:, None, :], jnp.sin(turned)[:, None, :])


def contract_rows(left_side, right_side):
    return lax.dot_general(
        left_side, right_side, (((0,), (0,)), ((), ())), preferred_element_type=F32
    )


def contract_cols(left_side, right_side):
    return lax.dot_general(
        left_side, right_side, (((1,), (1,)), ((), ())), preferred_element_type=F32
    )


def swap(value):
    return lax.ppermute(value, "shard", [(0, 1), (1, 0)])


def mlp_up_kernel(s_ref, bo_ref, bx_ref, go_ref, uo_ref, gx_ref, ux_ref, gate_ref, up_ref, m_ref):
    gate = jnp.dot(bo_ref[...], go_ref[0], preferred_element_type=F32)
    gate += jnp.dot(bx_ref[...], gx_ref[0], preferred_element_type=F32)
    up = jnp.dot(bo_ref[...], uo_ref[0], preferred_element_type=F32)
    up += jnp.dot(bx_ref[...], ux_ref[0], preferred_element_type=F32)
    gate_ref[...] = gate
    up_ref[...] = up
    m_ref[...] = (gate * jax.nn.sigmoid(gate) * up).astype(BF)


def w_specs(layer):
    return [
        pl.BlockSpec((1, HALF, FH), lambda i, s, l=layer: (l, 0, s[0])),
        pl.BlockSpec((1, HALF, FH), lambda i, s, l=layer: (l, 0, 2 + s[0])),
    ]


def whole(shape):
    return pl.BlockSpec(shape, lambda i, s: (0,) * len(shape))


def mlp_up(s, b_own, b_oth, w_own, w_oth, layer):
    rows = b_own.shape[0]
    return pl.pallas_call(
        mlp_up_kernel,
        grid_spec=pltpu.PrefetchScalarGridSpec(
            num_scalar_prefetch=1,
            grid=(1,),
            in_specs=[whole((rows, HALF)), whole((rows, HALF))] + w_specs(layer) + w_specs(0),
            out_specs=[whole((rows, FH)), whole((rows, FH)), whole((rows, FH))],
        ),
        out_shape=[
            jax.ShapeDtypeStruct((rows, FH), F32),
            jax.ShapeDtypeStruct((rows, FH), F32),
            jax.ShapeDtypeStruct((rows, FH), BF),
        ],
        compiler_params=pltpu.CompilerParams(vmem_limit_bytes=VMEM),
        cost_estimate=pl.CostEstimate(
            flops=4 * rows * D * FH, bytes_accessed=14_500_000, transcendentals=rows * FH
        ),
        name="mlp_up",
    )(s, b_own, b_oth, w_own, w_own, w_oth, w_oth)


def mlp_back_kernel(
    s_ref, df_ref, wd_ref, gate_ref, up_ref, go_ref, uo_ref, gx_ref, ux_ref, dgu_ref, dbo_ref, dbx_ref
):
    dm = contract_cols(df_ref[...], wd_ref[0])
    gate = gate_ref[...]
    sig = jax.nn.sigmoid(gate)
    act = gate * sig
    dup = (dm * act).astype(BF)
    dgate = (dm * up_ref[...] * (sig * (1.0 + gate * (1.0 - sig)))).astype(BF)
    dgu_ref[:, :FH] = dgate
    dgu_ref[:, FH:] = dup
    dbo_ref[...] = contract_cols(dgate, go_ref[0]) + contract_cols(dup, uo_ref[0])
    dbx_ref[...] = contract_cols(dgate, gx_ref[0]) + contract_cols(dup, ux_ref[0])


def mlp_back(s, df, w_down, gate, up, w_own, w_oth, layer):
    rows = df.shape[0]
    return pl.pallas_call(
        mlp_back_kernel,
        grid_spec=pltpu.PrefetchScalarGridSpec(
            num_scalar_prefetch=1,
            grid=(1,),
            in_specs=[
                whole((rows, D)),
                pl.BlockSpec((1, FH, D), lambda i, s, l=layer: (l, 0, 0)),
                whole((rows, FH)),
                whole((rows, FH)),
            ]
            + w_specs(layer)
            + w_specs(0),
            out_specs=[whole((rows, 2 * FH)), whole((rows, HALF)), whole((rows, HALF))],
        ),
        out_shape=[
            jax.ShapeDtypeStruct((rows, 2 * FH), BF),
            jax.ShapeDtypeStruct((rows, HALF), F32),
            jax.ShapeDtypeStruct((rows, HALF), F32),
        ],
        compiler_params=pltpu.CompilerParams(vmem_limit_bytes=VMEM),
        cost_estimate=pl.CostEstimate(
            flops=6 * rows * D * FH, bytes_accessed=23_000_000, transcendentals=rows * FH
        ),
        name="mlp_back",
    )(s, df, w_down, gate, up, w_own, w_own, w_oth, w_oth)


def grad_gu_kernel(s_ref, b_ref, own_ref, oth_ref, out_ref):
    mine = lax.rem(pl.program_id(0), 2) == s_ref[0]

    @pl.when(mine)
    def _():
        out_ref[...] = contract_rows(b_ref[0], own_ref[...]).astype(BF)

    @pl.when(jnp.logical_not(mine))
    def _():
        out_ref[...] = contract_rows(b_ref[1], oth_ref[...]).astype(BF)


def grad_gu(s, b_pair, dgu_own, dgu_oth):
    rows = dgu_own.shape[0]
    return pl.pallas_call(
        grad_gu_kernel,
        grid_spec=pltpu.PrefetchScalarGridSpec(
            num_scalar_prefetch=1,
            grid=(4,),
            in_specs=[
                whole((2, rows, HALF)),
                pl.BlockSpec((rows, FH), lambda i, s: (0, i // 2)),
                pl.BlockSpec((rows, FH), lambda i, s: (0, i // 2)),
            ],
            out_specs=pl.BlockSpec((HALF, FH), lambda i, s: (0, i)),
        ),
        out_shape=jax.ShapeDtypeStruct((HALF, 2 * FF), BF),
        compiler_params=pltpu.CompilerParams(vmem_limit_bytes=VMEM),
        cost_estimate=pl.CostEstimate(
            flops=4 * rows * HALF * FF, bytes_accessed=14_000_000, transcendentals=0
        ),
        name="grad_gu",
    )(s, b_pair, dgu_own, dgu_oth)


def body(
    hidden_in,
    seq_lengths,
    block_owner,
    norm_attn,
    w_qkv,
    b_qkv,
    w_out,
    norm_mlp,
    w_gate_up,
    w_down,
    grad_out,
):
    layer_count = 2
    width_q = HEADS * HEAD
    width_k = KV_HEADS * HEAD
    per_group = HEADS // KV_HEADS
    scale_factor = HEAD ** (-0.5)
    me = lax.axis_index("shard")
    first = me == 0
    s_arr = me.astype(jnp.int32).reshape(1)

    def pick(low, high):
        return jnp.where(first, low, high)

    def own_half(value, size):
        return pick(value[..., :size], value[..., size:])

    def other_half(value, size):
        return pick(value[..., size:], value[..., :size])

    def join(mine, theirs, axis):
        return pick(
            jnp.concatenate([mine, theirs], axis=axis), jnp.concatenate([theirs, mine], axis=axis)
        )

    lengths = seq_lengths[0]
    owner_row = block_owner[0]
    offsets = jnp.arange(TOK, dtype=jnp.int32)
    my_stream = owner_row[me] * TOK + offsets
    key_stream = jnp.concatenate([my_stream, owner_row[1 - me] * TOK + offsets])
    key_docs, key_pos = doc_position(key_stream, lengths)
    my_docs, positions = doc_position(my_stream, lengths)
    allowed = (my_docs[:, None] == key_docs[None, :]) & (key_stream[None, :] <= my_stream[:, None])
    cosine, sine_part = angles(positions, HEAD)

    small_own = jnp.concatenate([norm_attn, b_qkv, norm_mlp], axis=1)
    small_oth = swap(small_own)
    gains_attn = join(small_own[:, :HALF], small_oth[:, :HALF], 1).astype(F32)
    biases = join(small_own[:, HALF:-HALF], small_oth[:, HALF:-HALF], 1).astype(F32)
    gains_mlp = join(small_own[:, -HALF:], small_oth[:, -HALF:], 1).astype(F32)
    w_proj, w_attn_out, w_gu_oth = [], [], []
    for layer in range(layer_count):
        w_proj.append(join(w_qkv[layer], swap(w_qkv[layer]), 0))
        w_attn_out.append(join(w_out[layer], swap(w_out[layer]), 0))
        w_gu_oth.append(swap(w_gate_up[layer : layer + 1]))

    def attn_scores(grouped, all_keys):
        raw_scores = (
            jnp.einsum("qcgd,kcd->cgqk", grouped, all_keys, preferred_element_type=F32)
            * scale_factor
        )
        return jnp.where(allowed, raw_scores, -1e30)

    residual = hidden_in.astype(F32)
    kept_state = []
    for layer in range(layer_count):
        normed = rms_scale(residual, gains_attn[layer]).astype(BF)
        normed_oth = swap(other_half(normed, HALF))
        projected = jnp.dot(normed, w_proj[layer], preferred_element_type=F32) + biases[layer]
        queries = rotate(projected[:, :width_q].reshape(-1, HEADS, HEAD), cosine, sine_part).astype(
            BF
        )
        rot_keys = rotate(
            projected[:, width_q : width_q + width_k].reshape(-1, KV_HEADS, HEAD), cosine, sine_part
        ).astype(BF)
        values = projected[:, width_q + width_k :].astype(BF)
        kv = jnp.concatenate([rot_keys.reshape(-1, width_k), values], axis=1)
        key_vals = jnp.concatenate([kv, swap(kv)], axis=0)
        all_keys = key_vals[:, :width_k].reshape(-1, KV_HEADS, HEAD)
        all_values = key_vals[:, width_k:].reshape(-1, KV_HEADS, HEAD)
        grouped = queries.reshape(-1, KV_HEADS, per_group, HEAD)
        scores = attn_scores(grouped, all_keys)
        row_max = jnp.max(scores, axis=-1, keepdims=True)
        exp_scores = jnp.exp(scores - row_max)
        row_sum = jnp.sum(exp_scores, axis=-1, keepdims=True)
        attn_probs = (exp_scores / row_sum).astype(BF)
        log_total = row_max + jnp.log(row_sum)
        attn_mixed = (
            jnp.einsum("cgqk,kcd->qcgd", attn_probs, all_values, preferred_element_type=F32)
            .reshape(-1, width_q)
            .astype(BF)
        )
        mixed_oth = swap(other_half(attn_mixed, HALF))
        middle = residual + jnp.dot(attn_mixed, w_attn_out[layer], preferred_element_type=F32)
        normed_mlp = rms_scale(middle, gains_mlp[layer]).astype(BF)
        normed_cat = jnp.concatenate([normed_mlp, swap(normed_mlp)], axis=0)
        b_own = own_half(normed_cat, HALF)
        b_oth = other_half(normed_cat, HALF)
        gate, up, hidden = mlp_up(s_arr, b_own, b_oth, w_gate_up, w_gu_oth[layer], layer)
        partial = jnp.dot(hidden, w_down[layer], preferred_element_type=F32)
        kept_state.append(
            (
                residual,
                normed,
                normed_oth,
                grouped,
                all_keys,
                all_values,
                log_total,
                attn_mixed,
                mixed_oth,
                middle,
                b_own,
                gate,
                up,
                hidden,
            )
        )
        residual = middle + partial[:TOK] + swap(partial[TOK:])

    grad_resid = grad_out
    collected = [None] * layer_count
    for layer in reversed(range(layer_count)):
        (
            resid_in,
            normed,
            normed_oth,
            grouped,
            all_keys,
            all_values,
            log_total,
            attn_mixed,
            mixed_oth,
            middle,
            b_own,
            gate,
            up,
            hidden,
        ) = kept_state[layer]
        out_grad = grad_resid.astype(BF)
        out_cat = jnp.concatenate([out_grad, swap(out_grad)], axis=0)
        dgu, db_own, db_oth = mlp_back(
            s_arr, out_cat, w_down, gate, up, w_gate_up, w_gu_oth[layer], layer
        )
        grad_down = contract_rows(hidden, out_cat).astype(BF)
        dgu_oth = swap(dgu)
        b_pair = jnp.stack([b_own, jnp.concatenate([b_own[TOK:], b_own[:TOK]], axis=0)])
        grad_wgu = grad_gu(s_arr, b_pair, dgu, dgu_oth)
        db = join(db_own, db_oth, 1)
        grad_normed_mlp = db[:TOK] + swap(db[TOK:])
        unused_out, norm_pull = jax.vjp(rms_scale, middle, gains_mlp[layer])
        grad_mid_norm, grad_gain_mlp = norm_pull(grad_normed_mlp)
        grad_middle = grad_resid + grad_mid_norm
        branch_grad = grad_middle.astype(BF)
        branch_cat = jnp.concatenate([branch_grad, swap(branch_grad)], axis=0)
        mixed_cat = jnp.concatenate([own_half(attn_mixed, HALF), mixed_oth], axis=0)
        grad_wo = contract_rows(mixed_cat, branch_cat).astype(BF)
        grad_mixed = (
            contract_cols(branch_grad, w_attn_out[layer])
            .astype(BF)
            .reshape(-1, KV_HEADS, per_group, HEAD)
        )
        scores = attn_scores(grouped, all_keys)
        probs_full = jnp.where(allowed, jnp.exp(scores - log_total), 0.0)
        grad_probs = jnp.einsum(
            "qcgd,kcd->cgqk", grad_mixed, all_values, preferred_element_type=F32
        )
        grad_values = jnp.einsum(
            "cgqk,qcgd->kcd", probs_full.astype(BF), grad_mixed, preferred_element_type=F32
        )
        row_dot = jnp.sum(probs_full * grad_probs, axis=-1, keepdims=True)
        grad_scores = (probs_full * (grad_probs - row_dot)).astype(BF)
        grad_queries = (
            jnp.einsum("cgqk,kcd->qcgd", grad_scores, all_keys, preferred_element_type=F32)
            * scale_factor
        )
        grad_keys = (
            jnp.einsum("cgqk,qcgd->kcd", grad_scores, grouped, preferred_element_type=F32)
            * scale_factor
        )
        key_terms = jnp.concatenate(
            [grad_keys.reshape(-1, width_k), grad_values.reshape(-1, width_k)], axis=1
        )
        own_keys = key_terms[:TOK] + swap(key_terms[TOK:])
        grad_q_pre = rotate(grad_queries.reshape(-1, HEADS, HEAD), cosine, -sine_part).reshape(
            -1, width_q
        )
        grad_k_pre = rotate(
            own_keys[:, :width_k].reshape(-1, KV_HEADS, HEAD), cosine, -sine_part
        ).reshape(-1, width_k)
        grad_proj = jnp.concatenate([grad_q_pre, grad_k_pre, own_keys[:, width_k:]], axis=1).astype(
            BF
        )
        proj_cat = jnp.concatenate([grad_proj, swap(grad_proj)], axis=0)
        normed_cat = jnp.concatenate([own_half(normed, HALF), normed_oth], axis=0)
        grad_wq = contract_rows(normed_cat, proj_cat).astype(BF)
        grad_bias = own_half(jnp.sum(proj_cat.astype(F32), axis=0), QKV // 2)
        grad_normed = contract_cols(grad_proj, w_proj[layer])
        unused_out, norm_pull = jax.vjp(rms_scale, resid_in, gains_attn[layer])
        grad_in_norm, grad_gain_attn = norm_pull(grad_normed)
        grad_resid = grad_middle + grad_in_norm
        gains = jnp.stack([grad_gain_attn, grad_gain_mlp])
        gains = own_half(gains, HALF) + swap(other_half(gains, HALF))
        vectors = jnp.concatenate([gains[0], gains[1], grad_bias]).astype(BF)
        collected[layer] = (vectors, grad_wq, grad_wo, grad_wgu, grad_down)
    summed = lax.psum(collected, "rep")
    members = [
        jnp.stack([summed[index][member].astype(F32) for index in range(layer_count)])
        for member in range(5)
    ]
    vectors = members[0]
    return (
        residual.astype(BF),
        grad_resid,
        vectors[:, :HALF],
        members[1],
        vectors[:, 2 * HALF :],
        members[2],
        vectors[:, HALF : 2 * HALF],
        members[3],
        members[4],
    )


def solution(mesh):
    placed = (
        P(("rep", "shard"), None),
        P("rep", None),
        P("rep", None),
        P(None, "shard"),
        P(None, "shard", None),
        P(None, "shard"),
        P(None, "shard", None),
        P(None, "shard"),
        P(None, "shard", None),
        P(None, "shard", None),
        P(("rep", "shard"), None),
    )
    return jax.shard_map(
        body,
        mesh=mesh,
        in_specs=placed,
        out_specs=(
            P(("rep", "shard"), None),
            P(("rep", "shard"), None),
            P(None, "shard"),
            P(None, "shard", None),
            P(None, "shard"),
            P(None, "shard", None),
            P(None, "shard"),
            P(None, "shard", None),
            P(None, "shard", None),
        ),
        check_vma=False,
    )
```

```python
import functools

import jax
import jax.numpy as jnp
from jax import lax
from jax.experimental import pallas as pl
from jax.experimental.pallas import tpu as pltpu
from jax.sharding import PartitionSpec as P

HEADS = 14
KV_HEADS = 2
HEAD = 64
D = 896
HALF = 448
FF = 4864
FH = 2432
QKV = 1152
TOK = 128
TILE = 16
CHUNK = 19
GU_TILES = 28 * CHUNK
DOWN_TILES = 56 * CHUNK
REST_TILES = 24 * CHUNK
TILES = 192 * CHUNK

epsilon = 1e-06
base_freq = 1000000.0
VMEM = 60 * 1024 * 1024
F32 = jnp.float32
BF = jnp.bfloat16


def doc_position(stream, lengths):
    doc_ends = jnp.cumsum(lengths)
    doc_ids = jnp.sum((stream[:, None] >= doc_ends[None, :]).astype(jnp.int32), axis=1)
    starts = jnp.max(jnp.where(doc_ends[None, :] <= stream[:, None], doc_ends[None, :], 0), axis=1)
    return (doc_ids, stream - starts)


def angles(positions, head_size):
    half_width = head_size // 2
    frequency = jnp.power(base_freq, -(jnp.arange(half_width, dtype=F32) * 2.0 / head_size))
    turned = positions.astype(F32)[:, None] * frequency[None, :]
    return (jnp.cos(turned), jnp.sin(turned))


def contract_rows(left_side, right_side):
    return lax.dot_general(
        left_side, right_side, (((0,), (0,)), ((), ())), preferred_element_type=F32
    )


def contract_cols(left_side, right_side):
    return lax.dot_general(
        left_side, right_side, (((1,), (1,)), ((), ())), preferred_element_type=F32
    )


def swap(value):
    return lax.ppermute(value, "shard", [(0, 1), (1, 0)])


def run(kernel, ins, outs, scratch=(), flops=0, name=None):
    arrays, specs = [], []
    for item in ins:
        if isinstance(item, tuple):
            array, kind = item
            specs.append(pl.BlockSpec(memory_space=kind))
        else:
            array = item
            specs.append(pl.BlockSpec(memory_space=pltpu.VMEM))
        arrays.append(array)
    moved = sum(x.size * x.dtype.itemsize for x in arrays if x.size < 4_000_000)
    moved += sum(4 * x[0][0] * x[0][1] for x in outs)
    return pl.pallas_call(
        kernel,
        in_specs=specs,
        out_specs=[pl.BlockSpec(memory_space=pltpu.VMEM)] * len(outs),
        out_shape=[jax.ShapeDtypeStruct(shape, kind) for shape, kind in outs],
        scratch_shapes=list(scratch),
        compiler_params=pltpu.CompilerParams(vmem_limit_bytes=VMEM),
        cost_estimate=pl.CostEstimate(flops=flops, bytes_accessed=moved, transcendentals=0),
        name=name,
    )(*arrays)


def halves(s, own_ref, oth_ref, place, sems, first_sem, layer, columns=None):
    cols = slice(None) if columns is None else pl.ds(pl.multiple_of(columns, 128), FH)
    copies = []
    for k, (ref, half) in enumerate(((own_ref, s), (oth_ref, 1 - s))):
        rows = pl.ds(pl.multiple_of(half * HALF, 64), HALF)
        copies.append(
            pltpu.make_async_copy(
                ref.at[layer, :, cols], place.at[rows, :], sems.at[first_sem + k]
            )
        )
    return copies


def start(copies):
    for copy in copies:
        copy.start()


def wait(copies):
    for copy in copies:
        copy.wait()


def rms_parts(values):
    return lax.rsqrt(jnp.mean(values * values, axis=1, keepdims=True) + epsilon)


def rms_back(values, gain, grad):
    r = rms_parts(values)
    scaled = grad * gain
    back = r * scaled - values * (r * r * r * jnp.mean(values * scaled, axis=1, keepdims=True))
    return back, jnp.sum(grad * values * r, axis=0, keepdims=True)


def turn(values, cosine, sine):
    width = values.shape[1]
    times = width // 128
    lane = lax.broadcasted_iota(jnp.int32, values.shape, 1)
    partner = jnp.where(
        lane % HEAD < HEAD // 2,
        pltpu.roll(values, width - HEAD // 2, 1),
        pltpu.roll(values, HEAD // 2, 1),
    )
    cosine = jnp.concatenate([cosine] * times, axis=1)
    sine = jnp.concatenate([sine] * times, axis=1)
    return values * cosine + partner * sine


def take_half(value, mine):
    return jnp.where(mine == 0, value[:, :HALF], value[:, HALF:])


def qkv_kernel(
    layer, s_ref, x_ref, gain_ref, bias_ref, cos_ref, sin_ref, wo_ref, wx_ref,
    own_ref, oth_ref, q_ref, kv_ref, w, sems,
):
    s = s_ref[0]
    copies = halves(s, wo_ref, wx_ref, w, sems, 0, layer)
    start(copies)
    x = x_ref[...]
    normed = x * rms_parts(x) * gain_ref[...]
    own_ref[...] = take_half(normed, s).astype(BF)
    oth_ref[...] = take_half(normed, 1 - s).astype(BF)
    wait(copies)
    proj = jnp.dot(normed.astype(BF), w[...], preferred_element_type=F32) + bias_ref[...]
    turned = turn(proj[:, : D + 128], cos_ref[...], sin_ref[...]).astype(BF)
    q_ref[...] = turned[:, :D]
    kv_ref[:, :128] = turned[:, D:]
    kv_ref[:, 128:] = proj[:, D + 128 :].astype(BF)


def qkv(s, layer, x, gain, bias, cos, sin, w_own, w_oth):
    return run(
        functools.partial(qkv_kernel, layer),
        [(s, pltpu.SMEM), x, gain, bias, cos, sin, (w_own, pl.ANY), (w_oth, pl.ANY)],
        [((TOK, HALF), BF), ((TOK, HALF), BF), ((TOK, D), BF), ((TOK, 256), BF)],
        [pltpu.VMEM((D, QKV), BF), pltpu.SemaphoreType.DMA((2,))],
        flops=2 * TOK * D * QKV,
        name="qkv",
    )


def head(values, index):
    return values[:, index * HEAD : (index + 1) * HEAD]


def keys_values(kvo_ref, kvx_ref):
    kv = jnp.concatenate([kvo_ref[...], kvx_ref[...]], axis=0)
    return [head(kv, c) for c in range(KV_HEADS)], [head(kv, KV_HEADS + c) for c in range(KV_HEADS)]


def attn_kernel(
    layer, s_ref, q_ref, kvo_ref, kvx_ref, ok_ref, x_ref, gain_ref, wo_ref, wx_ref,
    own_ref, oth_ref, lse_ref, mid_ref, b_ref, w, mixed, sems,
):
    s = s_ref[0]
    copies = halves(s, wo_ref, wx_ref, w, sems, 0, layer)
    start(copies)
    keys, values = keys_values(kvo_ref, kvx_ref)
    allowed = ok_ref[...] > 0.0
    for h in range(HEADS):
        c = h * KV_HEADS // HEADS
        scores = contract_cols(head(q_ref, h), keys[c]) * HEAD**-0.5
        scores = jnp.where(allowed, scores, -1e30)
        top = jnp.max(scores, axis=1, keepdims=True)
        raised = jnp.exp(scores - top)
        total = jnp.sum(raised, axis=1, keepdims=True)
        probs = (raised / total).astype(BF)
        lse_ref[h] = top + jnp.log(total)
        mixed[:, h * HEAD : (h + 1) * HEAD] = jnp.dot(
            probs, values[c], preferred_element_type=F32
        )
    o = mixed[...]
    own_ref[...] = take_half(o, s).astype(BF)
    oth_ref[...] = take_half(o, 1 - s).astype(BF)
    wait(copies)
    middle = x_ref[...] + jnp.dot(o.astype(BF), w[...], preferred_element_type=F32)
    mid_ref[...] = middle
    b_ref[...] = (middle * rms_parts(middle) * gain_ref[...]).astype(BF)


def attn(s, layer, q, kv, kv_oth, allowed, x, gain, w_own, w_oth):
    return run(
        functools.partial(attn_kernel, layer),
        [(s, pltpu.SMEM), q, kv, kv_oth, allowed, x, gain, (w_own, pl.ANY), (w_oth, pl.ANY)],
        [
            ((TOK, HALF), BF),
            ((TOK, HALF), BF),
            ((HEADS, TOK, 1), F32),
            ((TOK, D), F32),
            ((TOK, D), BF),
        ],
        [pltpu.VMEM((D, D), BF), pltpu.VMEM((TOK, D), F32), pltpu.SemaphoreType.DMA((2,))],
        flops=2 * TOK * D * D + 4 * TOK * 256 * D,
        name="attn",
    )


def mlp_up_kernel(
    layer, s_ref, b_ref, bx_ref, gu_ref, gux_ref, wd_ref,
    own_ref, gate_ref, up_ref, m_ref, mine_ref, theirs_ref, wg, wu, wd, sems,
):
    s = s_ref[0]
    gates = halves(s, gu_ref, gux_ref, wg, sems, 0, layer, s * FH)
    ups = halves(s, gu_ref, gux_ref, wu, sems, 2, layer, FF + s * FH)
    down = [pltpu.make_async_copy(wd_ref.at[layer], wd, sems.at[4])]
    start(gates + ups + down)
    b = jnp.concatenate([b_ref[...], bx_ref[...]], axis=0)
    own_ref[...] = take_half(b.astype(F32), s).astype(BF)
    wait(gates)
    gate_ref[...] = jnp.dot(b, wg[...], preferred_element_type=F32)
    wait(ups)
    up_ref[...] = jnp.dot(b, wu[...], preferred_element_type=F32)
    gate = gate_ref[...]
    m_ref[...] = (gate * jax.nn.sigmoid(gate) * up_ref[...]).astype(BF)
    wait(down)
    partial = jnp.dot(m_ref[...], wd[...], preferred_element_type=F32)
    mine_ref[...] = partial[:TOK]
    theirs_ref[...] = partial[TOK:]


WEIGHTS = (
    pltpu.VMEM((D, FH), BF),
    pltpu.VMEM((D, FH), BF),
    pltpu.VMEM((FH, D), BF),
    pltpu.SemaphoreType.DMA((5,)),
)


def mlp_up(s, layer, b, b_oth, w_own, w_oth, w_down):
    rows = 2 * TOK
    return run(
        functools.partial(mlp_up_kernel, layer),
        [(s, pltpu.SMEM), b, b_oth, (w_own, pl.ANY), (w_oth, pl.ANY), (w_down, pl.ANY)],
        [
            ((rows, HALF), BF),
            ((rows, FH), F32),
            ((rows, FH), F32),
            ((rows, FH), BF),
            ((TOK, D), F32),
            ((TOK, D), F32),
        ],
        WEIGHTS,
        flops=6 * rows * D * FH,
        name="mlp_up",
    )


def mlp_back_kernel(
    layer, s_ref, df_ref, dfx_ref, gate_ref, up_ref, gu_ref, gux_ref, wd_ref,
    dgu_ref, mine_ref, theirs_ref, wg, wu, wd, sems,
):
    s = s_ref[0]
    gates = halves(s, gu_ref, gux_ref, wg, sems, 0, layer, s * FH)
    ups = halves(s, gu_ref, gux_ref, wu, sems, 2, layer, FF + s * FH)
    down = [pltpu.make_async_copy(wd_ref.at[layer], wd, sems.at[4])]
    start(down + gates + ups)
    df = jnp.concatenate([df_ref[...], dfx_ref[...]], axis=0)
    wait(down)
    dm = contract_cols(df, wd[...])
    gate = gate_ref[...]
    sig = jax.nn.sigmoid(gate)
    dgu_ref[:, FH:] = (dm * gate * sig).astype(BF)
    dgu_ref[:, :FH] = (dm * up_ref[...] * (sig * (1.0 + gate * (1.0 - sig)))).astype(BF)
    wait(gates)
    db = contract_cols(dgu_ref[:, :FH], wg[...])
    wait(ups)
    db += contract_cols(dgu_ref[:, FH:], wu[...])
    mine_ref[...] = db[:TOK]
    theirs_ref[...] = db[TOK:]


def mlp_back(s, layer, df, df_oth, gate, up, w_own, w_oth, w_down):
    rows = 2 * TOK
    return run(
        functools.partial(mlp_back_kernel, layer),
        [(s, pltpu.SMEM), df, df_oth, gate, up]
        + [(w_own, pl.ANY), (w_oth, pl.ANY), (w_down, pl.ANY)],
        [((rows, 2 * FH), BF), ((TOK, D), F32), ((TOK, D), F32)],
        WEIGHTS,
        flops=6 * rows * D * FH,
        name="mlp_back",
    )


def attn_back_kernel(
    layer, s_ref, g_ref, db_ref, dbx_ref, mid_ref, gain_ref, q_ref, kvo_ref, kvx_ref, ok_ref,
    lse_ref, cos_ref, sin_ref, wo_ref, wx_ref,
    dh_ref, da_ref, dq_ref, mine_ref, theirs_ref, dgain_ref, w, dq, sems,
):
    s = s_ref[0]
    copies = halves(s, wo_ref, wx_ref, w, sems, 0, layer)
    start(copies)
    back, dgain_ref[...] = rms_back(mid_ref[...], gain_ref[...], db_ref[...] + dbx_ref[...])
    dh = g_ref[...] + back
    dh_ref[...] = dh
    da = dh.astype(BF)
    da_ref[...] = da
    wait(copies)
    do = contract_cols(da, w[...]).astype(BF)
    keys, values = keys_values(kvo_ref, kvx_ref)
    allowed = ok_ref[...] > 0.0
    dk = [jnp.zeros((2 * TOK, HEAD), F32) for c in range(KV_HEADS)]
    dv = [jnp.zeros((2 * TOK, HEAD), F32) for c in range(KV_HEADS)]
    for h in range(HEADS):
        c = h * KV_HEADS // HEADS
        q_h, do_h = head(q_ref, h), head(do, h)
        scores = contract_cols(q_h, keys[c]) * HEAD**-0.5
        probs = jnp.where(allowed, jnp.exp(scores - lse_ref[h]), 0.0)
        dp = contract_cols(do_h, values[c])
        dv[c] += contract_rows(probs.astype(BF), do_h)
        row_dot = jnp.sum(probs * dp, axis=1, keepdims=True)
        ds = (probs * (dp - row_dot)).astype(BF)
        dq[:, h * HEAD : (h + 1) * HEAD] = (
            jnp.dot(ds, keys[c], preferred_element_type=F32) * HEAD**-0.5
        )
        dk[c] += contract_rows(ds, q_h) * HEAD**-0.5
    dq_ref[...] = turn(dq[...], cos_ref[...], -sin_ref[...]).astype(BF)
    dkv = jnp.concatenate(dk + dv, axis=1)
    mine_ref[...] = dkv[:TOK]
    theirs_ref[...] = dkv[TOK:]


def attn_back(s, layer, g, db, db_oth, mid, gain, q, kv, kv_oth, ok, lse, cos, sin, w_own, w_oth):
    return run(
        functools.partial(attn_back_kernel, layer),
        [(s, pltpu.SMEM), g, db, db_oth, mid, gain, q, kv, kv_oth, ok, lse, cos, sin]
        + [(w_own, pl.ANY), (w_oth, pl.ANY)],
        [
            ((TOK, D), F32),
            ((TOK, D), BF),
            ((TOK, D), BF),
            ((TOK, 256), F32),
            ((TOK, 256), F32),
            ((1, D), F32),
        ],
        [pltpu.VMEM((D, D), BF), pltpu.VMEM((TOK, D), F32), pltpu.SemaphoreType.DMA((2,))],
        flops=2 * TOK * D * D + 10 * TOK * 256 * D,
        name="attn_back",
    )


def qkv_back_kernel(
    layer, s_ref, dq_ref, dkv_ref, dkvx_ref, dh_ref, x_ref, gain_ref, cos_ref, sin_ref, wo_ref, wx_ref,
    dproj_ref, g_ref, gb_ref, dgain_ref, w, sems,
):
    s = s_ref[0]
    copies = halves(s, wo_ref, wx_ref, w, sems, 0, layer)
    start(copies)
    dkv = dkv_ref[...] + dkvx_ref[...]
    dproj_ref[:, :D] = dq_ref[...]
    dproj_ref[:, D : D + 128] = turn(dkv[:, :128], cos_ref[...], -sin_ref[...]).astype(BF)
    dproj_ref[:, D + 128 :] = dkv[:, 128:].astype(BF)
    wait(copies)
    da = contract_cols(dproj_ref[...], w[...])
    back, dgain_ref[...] = rms_back(x_ref[...], gain_ref[...], da)
    g = dh_ref[...] + back
    g_ref[...] = g
    gb_ref[...] = g.astype(BF)


def qkv_back(s, layer, dq, dkv, dkv_oth, dh, x, gain, cos, sin, w_own, w_oth):
    return run(
        functools.partial(qkv_back_kernel, layer),
        [(s, pltpu.SMEM), dq, dkv, dkv_oth, dh, x, gain, cos, sin]
        + [(w_own, pl.ANY), (w_oth, pl.ANY)],
        [((TOK, QKV), BF), ((TOK, D), F32), ((TOK, D), BF), ((1, D), F32)],
        [pltpu.VMEM((D, QKV), BF), pltpu.SemaphoreType.DMA((2,))],
        flops=2 * TOK * D * QKV,
        name="qkv_back",
    )


def whole(shape):
    return pl.BlockSpec(shape, lambda i, s: (0,) * len(shape))


def store_columns(out_ref, at, value):
    high = value.shape[0] // TILE
    for c in range(value.shape[1] // 128):
        piece = value[:, c * 128 : (c + 1) * 128].reshape(high, TILE, 128)
        out_ref[at + c * high : at + (c + 1) * high] = piece.astype(BF)


def grad_gu_kernel(s_ref, b_ref, own_ref, oth_ref, out_ref):
    mine = lax.rem(pl.program_id(0), 2) == s_ref[0]

    @pl.when(mine)
    def _():
        store_columns(out_ref, 0, contract_rows(b_ref[...], own_ref[...]))

    @pl.when(jnp.logical_not(mine))
    def _():
        turned = jnp.concatenate([b_ref[TOK:], b_ref[:TOK]], axis=0)
        store_columns(out_ref, 0, contract_rows(turned, oth_ref[...]))


def grad_gu(s, b, dgu_own, dgu_oth):
    rows = dgu_own.shape[0]
    return pl.pallas_call(
        grad_gu_kernel,
        grid_spec=pltpu.PrefetchScalarGridSpec(
            num_scalar_prefetch=1,
            grid=(4,),
            in_specs=[
                whole((rows, HALF)),
                pl.BlockSpec((rows, FH), lambda i, s: (0, i // 2)),
                pl.BlockSpec((rows, FH), lambda i, s: (0, i // 2)),
            ],
            out_specs=pl.BlockSpec((GU_TILES, TILE, 128), lambda i, s: (i, 0, 0)),
        ),
        out_shape=jax.ShapeDtypeStruct((TILES, TILE, 128), BF),
        compiler_params=pltpu.CompilerParams(vmem_limit_bytes=VMEM),
        cost_estimate=pl.CostEstimate(
            flops=4 * rows * HALF * FF, bytes_accessed=14_000_000, transcendentals=0
        ),
        name="grad_gu",
    )(s, b, dgu_own, dgu_oth)


def grad_down_kernel(m_ref, df_ref, dfx_ref, old_ref, out_ref):
    df = jnp.concatenate([df_ref[...], dfx_ref[...]], axis=0)
    store_columns(out_ref, 0, contract_rows(m_ref[...], df))


def grad_rest_kernel(
    a_ref, ax_ref, dp_ref, dpx_ref, o_ref, ox_ref, da_ref, dax_ref, vec_ref, old_ref, out_ref
):
    a = jnp.concatenate([a_ref[...], ax_ref[...]], axis=0)
    dp = jnp.concatenate([dp_ref[...], dpx_ref[...]], axis=0)
    store_columns(out_ref, 0, contract_rows(a, dp))
    o = jnp.concatenate([o_ref[...], ox_ref[...]], axis=0)
    da = jnp.concatenate([da_ref[...], dax_ref[...]], axis=0)
    store_columns(out_ref, 252, contract_rows(o, da))
    out_ref[448:] = vec_ref[...]


def fill(kernel, ins, packed, tiles, index, flops, name):
    return pl.pallas_call(
        kernel,
        grid=(1,),
        in_specs=[pl.BlockSpec(x.shape, lambda i, n=x.ndim: (0,) * n) for x in ins]
        + [pl.BlockSpec(memory_space=pl.ANY)],
        out_specs=pl.BlockSpec((tiles, TILE, 128), lambda i: (index, 0, 0)),
        out_shape=jax.ShapeDtypeStruct(packed.shape, BF),
        input_output_aliases={len(ins): 0},
        compiler_params=pltpu.CompilerParams(vmem_limit_bytes=VMEM),
        cost_estimate=pl.CostEstimate(
            flops=flops, bytes_accessed=2 * tiles * TILE * 128, transcendentals=0
        ),
        name=name,
    )(*ins, packed)


def chunk_copies(table_ref, from_ref, place, sem, first, count):
    def one(n, carry):
        tiles = pl.ds(n * CHUNK, CHUNK)
        pltpu.make_async_copy(from_ref.at[table_ref[n]], place.at[tiles], sem).start()
        return carry

    lax.fori_loop(first, first + count, one, 0)


def unpack_kernel(layer, olds, table_ref, from_ref, *refs):
    out_q, out_o, out_gu, out_d, vec_ref, place, stage_gu, stage_d, stage_q, stage_o, sems, out_sems = refs[olds:]
    for j in range(4):
        chunk_copies(table_ref, from_ref, place, sems.at[j], 28 * j, 28)
    chunk_copies(table_ref, from_ref, place, sems.at[4], 112, 56)
    chunk_copies(table_ref, from_ref, place, sems.at[5], 168, 24)

    def arrived(first, tiles, sem):
        part = place.at[first : first + tiles]
        pltpu.make_async_copy(part, part, sem).wait()

    def spread(stage, first):
        rows = stage.shape[0]
        high = rows // TILE
        for c in range(stage.shape[1] // 128):
            piece = place[first + c * high : first + (c + 1) * high]
            stage[:, c * 128 : (c + 1) * 128] = piece.astype(F32).reshape(rows, 128)

    sent = []
    for j in range(4):
        arrived(j * GU_TILES, GU_TILES, sems.at[j])
        if j >= 2:
            sent[j - 2].wait()
        spread(stage_gu.at[j % 2], j * GU_TILES)
        copy = pltpu.make_async_copy(
            stage_gu.at[j % 2], out_gu.at[layer, :, j * FH : (j + 1) * FH], out_sems.at[j]
        )
        copy.start()
        sent.append(copy)
    first = 4 * GU_TILES
    arrived(first, DOWN_TILES, sems.at[4])
    spread(stage_d, first)
    sent.append(pltpu.make_async_copy(stage_d, out_d.at[layer], out_sems.at[4]))
    sent[4].start()
    first += DOWN_TILES
    arrived(first, REST_TILES, sems.at[5])
    spread(stage_q, first)
    sent.append(pltpu.make_async_copy(stage_q, out_q.at[layer], out_sems.at[5]))
    sent[5].start()
    spread(stage_o, first + 252)
    sent.append(pltpu.make_async_copy(stage_o, out_o.at[layer], out_sems.at[6]))
    sent[6].start()
    vec_ref[...] = place[first + 448 : first + 456].astype(F32)
    for copy in sent[2:]:
        copy.wait()


def unpack(table, gathered, layer, olds):
    shapes = [(2, HALF, QKV), (2, HALF, D), (2, HALF, 2 * FF), (2, FH, D)]
    return pl.pallas_call(
        functools.partial(unpack_kernel, layer, len(olds)),
        in_specs=[pl.BlockSpec(memory_space=pltpu.SMEM)]
        + [pl.BlockSpec(memory_space=pl.ANY)] * (1 + len(olds)),
        out_specs=[pl.BlockSpec(memory_space=pl.ANY)] * 4 + [pl.BlockSpec(memory_space=pltpu.VMEM)],
        out_shape=[jax.ShapeDtypeStruct(shape, F32) for shape in shapes]
        + [jax.ShapeDtypeStruct((8, TILE, 128), F32)],
        input_output_aliases={2 + i: i for i in range(len(olds))},
        scratch_shapes=[
            pltpu.VMEM((TILES, TILE, 128), BF),
            pltpu.VMEM((2, HALF, FH), F32),
            pltpu.VMEM((FH, D), F32),
            pltpu.VMEM((HALF, QKV), F32),
            pltpu.VMEM((HALF, D), F32),
            pltpu.SemaphoreType.DMA((6,)),
            pltpu.SemaphoreType.DMA((7,)),
        ],
        compiler_params=pltpu.CompilerParams(vmem_limit_bytes=VMEM),
        cost_estimate=pl.CostEstimate(flops=0, bytes_accessed=45_000_000, transcendentals=0),
        name="unpack",
    )(table, gathered, *olds)


ORDERS = (("x", "y", "z"), ("y", "z", "x"), ("z", "x", "y"))
STRIDE = {"x": 1, "y": 4, "z": 16}


def pairing(axis, stage):
    pairs = []
    for rep in range(64):
        at = rep // STRIDE[axis] % 4
        for core in range(2):
            to = at ^ 1 if stage == core else 3 - at
            pairs.append((rep * 2 + core, (rep + (to - at) * STRIDE[axis]) * 2 + core))
    return pairs


def kept_half(rep, core, axis, stage):
    at = rep // STRIDE[axis] % 4
    if core == 0:
        return ((at + 1) // 2) % 2 if stage == 0 else at // 2
    return at // 2 if stage == 0 else at % 2


def all_steps(flow):
    return [(axis, stage) for axis in ORDERS[flow] for stage in (0, 1)]


def chunk_table(core):
    table = [0] * 192
    for rep in range(64):
        for flow in range(3):
            index = 0
            for axis, stage in all_steps(flow):
                index = index * 2 + kept_half(rep, core, axis, stage)
            table[flow * 64 + index] = rep * 3 + flow
    return jnp.array(table, jnp.int32)


def scatter_sum(packed):
    count = TILES // 3
    rep = lax.axis_index("rep")
    first = lax.axis_index("shard") == 0
    kept = [packed] * 3
    got = [None] * 3
    for step in range(7):
        half = count >> (step + 1)
        for flow in range(3):

            def part(start, size):
                if step == 0:
                    return lax.dynamic_slice_in_dim(packed, flow * count + start, size, 0)
                a = lax.dynamic_slice_in_dim(kept[flow], start, size, 0).astype(F32)
                b = lax.dynamic_slice_in_dim(got[flow], start, size, 0).astype(F32)
                return (a + b).astype(BF)

            if step == 6:
                kept[flow] = part(0, CHUNK)
                continue
            axis, stage = all_steps(flow)[step]
            keep = jnp.where(first, kept_half(rep, 0, axis, stage), kept_half(rep, 1, axis, stage))
            sent = part((1 - keep) * half, half)
            mine = part(keep * half, half)
            got[flow] = lax.ppermute(sent, ("rep", "shard"), pairing(axis, stage))
            kept[flow] = mine
    return jnp.concatenate(kept)


def gather_sum(chunks):
    gathered = lax.all_gather(chunks, "rep", axis=0, tiled=True)
    return gathered.reshape(192, CHUNK, TILE, 128)


def body(
    hidden_in,
    seq_lengths,
    block_owner,
    norm_attn,
    w_qkv,
    b_qkv,
    w_out,
    norm_mlp,
    w_gate_up,
    w_down,
    grad_out,
):
    layer_count = 2
    me = lax.axis_index("shard")
    first = me == 0
    s_arr = me.astype(jnp.int32).reshape(1)

    def own_half(value, size):
        return jnp.where(first, value[..., :size], value[..., size:])

    def other_half(value, size):
        return jnp.where(first, value[..., size:], value[..., :size])

    def join(mine, theirs):
        return jnp.where(
            first,
            jnp.concatenate([mine, theirs], axis=1),
            jnp.concatenate([theirs, mine], axis=1),
        ).astype(F32)

    small_own = jnp.concatenate([norm_attn, b_qkv, norm_mlp], axis=1)
    small_oth = swap(small_own)
    wq_oth = swap(w_qkv)
    wo_oth = swap(w_out)
    gu_oth = swap(w_gate_up)
    out_grad = grad_out.astype(BF)
    gains_attn = join(small_own[:, :HALF], small_oth[:, :HALF])
    biases = join(small_own[:, HALF:-HALF], small_oth[:, HALF:-HALF])
    gains_mlp = join(small_own[:, -HALF:], small_oth[:, -HALF:])

    lengths = seq_lengths[0]
    owner_row = block_owner[0]
    offsets = jnp.arange(TOK, dtype=jnp.int32)
    my_stream = owner_row[me] * TOK + offsets
    key_stream = jnp.concatenate([my_stream, owner_row[1 - me] * TOK + offsets])
    key_docs, key_pos = doc_position(key_stream, lengths)
    my_docs, positions = doc_position(my_stream, lengths)
    allowed = (my_docs[:, None] == key_docs[None, :]) & (key_stream[None, :] <= my_stream[:, None])
    allowed = allowed.astype(F32)
    cosine, sine_part = angles(positions, HEAD)
    cos = jnp.concatenate([cosine] * 4, axis=1)
    sin = jnp.concatenate([-sine_part, sine_part] * 2, axis=1)

    residual = hidden_in.astype(F32)
    kept_state = []
    for layer in range(layer_count):
        gain_a = gains_attn[layer : layer + 1]
        gain_m = gains_mlp[layer : layer + 1]
        a_own, a_send, q, kv = qkv(
            s_arr, layer, residual, gain_a, biases[layer : layer + 1], cos, sin, w_qkv, wq_oth
        )
        kv_oth = swap(kv)
        o_own, o_send, lse, middle, b = attn(
            s_arr, layer, q, kv, kv_oth, allowed, residual, gain_m, w_out, wo_oth
        )
        b_oth = swap(b)
        a_oth = swap(a_send)
        o_oth = swap(o_send)
        b_own, gate, up, hidden, mine, theirs = mlp_up(
            s_arr, layer, b, b_oth, w_gate_up, gu_oth, w_down
        )
        a_pair = (a_own, a_oth)
        o_pair = (o_own, o_oth)
        kept_state.append(
            (residual, a_pair, q, kv, kv_oth, lse, o_pair, middle, b_own, gate, up, hidden, gain_a, gain_m)
        )
        residual = middle + mine + swap(theirs)

    grad_resid = grad_out
    for layer in reversed(range(layer_count)):
        resid_in, a_pair, q, kv, kv_oth, lse, o_pair, middle, b_own, gate, up, hidden, gain_a, gain_m = (
            kept_state[layer]
        )
        out_oth = swap(out_grad)
        dgu, db, db_send = mlp_back(
            s_arr, layer, out_grad, out_oth, gate, up, w_gate_up, gu_oth, w_down
        )
        db_oth = swap(db_send)
        dgu_oth = swap(dgu)
        down_grad = (out_grad, out_oth)
        dh, da, dq, dkv, dkv_send, gain_m_grad = attn_back(
            s_arr, layer, grad_resid, db, db_oth, middle, gain_m, q, kv, kv_oth, allowed, lse,
            cos, sin, w_out, wo_oth,
        )
        dkv_oth = swap(dkv_send)
        da_oth = swap(da)
        dproj, grad_resid, out_grad, gain_a_grad = qkv_back(
            s_arr, layer, dq, dkv, dkv_oth, dh, resid_in, gain_a, cos, sin, w_qkv, wq_oth
        )
        dproj_oth = swap(dproj)
        grad_bias = jnp.sum(dproj.astype(F32), axis=0) + jnp.sum(dproj_oth.astype(F32), axis=0)
        gains = jnp.concatenate([gain_a_grad, gain_m_grad], axis=0)
        gains = own_half(gains, HALF) + swap(other_half(gains, HALF))
        vectors = jnp.concatenate([gains[0], gains[1], own_half(grad_bias, QKV // 2)])
        vectors = jnp.pad(vectors, (0, 8 * TILE * 128 - vectors.shape[0])).astype(BF)
        packed = grad_gu(s_arr, b_own, dgu, dgu_oth)
        packed = fill(
            grad_down_kernel, (hidden,) + down_grad, packed, DOWN_TILES, 2, 4 * TOK * FH * D, "grad_down"
        )
        packed = fill(
            grad_rest_kernel,
            a_pair + (dproj, dproj_oth) + o_pair + (da, da_oth) + (vectors.reshape(8, TILE, 128),),
            packed,
            REST_TILES,
            7,
            4 * TOK * HALF * (QKV + D),
            "grad_rest",
        )
        if layer == 1:
            grad_resid, out_grad, packed = lax.optimization_barrier((grad_resid, out_grad, packed))
            upper_sum = lax.psum(packed, "rep").reshape(192, CHUNK, TILE, 128)
        else:
            lower_chunks = scatter_sum(packed)
    table = jnp.where(first, chunk_table(0), chunk_table(1))
    *grads, upper = unpack(jnp.arange(192, dtype=jnp.int32), upper_sum, 1, [])
    *grads, lower = unpack(table, gather_sum(lower_chunks), 0, grads)
    vectors = jnp.stack([lower.reshape(-1)[:1472], upper.reshape(-1)[:1472]])
    return (
        residual.astype(BF),
        grad_resid,
        vectors[:, :HALF],
        grads[0],
        vectors[:, 2 * HALF :],
        grads[1],
        vectors[:, HALF : 2 * HALF],
        grads[2],
        grads[3],
    )


def solution(mesh):
    placed = (
        P(("rep", "shard"), None),
        P("rep", None),
        P("rep", None),
        P(None, "shard"),
        P(None, "shard", None),
        P(None, "shard"),
        P(None, "shard", None),
        P(None, "shard"),
        P(None, "shard", None),
        P(None, "shard", None),
        P(("rep", "shard"), None),
    )
    return jax.shard_map(
        body,
        mesh=mesh,
        in_specs=placed,
        out_specs=(
            P(("rep", "shard"), None),
            P(("rep", "shard"), None),
            P(None, "shard"),
            P(None, "shard", None),
            P(None, "shard"),
            P(None, "shard", None),
            P(None, "shard"),
            P(None, "shard", None),
            P(None, "shard", None),
        ),
        check_vma=False,
    )
```

```python
import functools

import jax
import jax.numpy as jnp
from jax import lax
from jax.experimental import pallas as pl
from jax.experimental.pallas import tpu as pltpu
from jax.sharding import PartitionSpec as P

HEADS = 14
KV_HEADS = 2
HEAD = 64
D = 896
HALF = 448
FF = 4864
FH = 2432
QKV = 1152
TOK = 128
TILE = 16
CHUNK = 19
GU_TILES = 28 * CHUNK
DOWN_TILES = 56 * CHUNK
REST_TILES = 24 * CHUNK
TILES = 192 * CHUNK

epsilon = 1e-06
base_freq = 1000000.0
VMEM = 60 * 1024 * 1024
F32 = jnp.float32
BF = jnp.bfloat16


def doc_position(stream, lengths):
    doc_ends = jnp.cumsum(lengths)
    doc_ids = jnp.sum((stream[:, None] >= doc_ends[None, :]).astype(jnp.int32), axis=1)
    starts = jnp.max(jnp.where(doc_ends[None, :] <= stream[:, None], doc_ends[None, :], 0), axis=1)
    return (doc_ids, stream - starts)


def angles(positions, head_size):
    half_width = head_size // 2
    frequency = jnp.power(base_freq, -(jnp.arange(half_width, dtype=F32) * 2.0 / head_size))
    turned = positions.astype(F32)[:, None] * frequency[None, :]
    return (jnp.cos(turned), jnp.sin(turned))


def contract_rows(left_side, right_side):
    return lax.dot_general(
        left_side, right_side, (((0,), (0,)), ((), ())), preferred_element_type=F32
    )


def contract_cols(left_side, right_side):
    return lax.dot_general(
        left_side, right_side, (((1,), (1,)), ((), ())), preferred_element_type=F32
    )


def swap(value):
    return lax.ppermute(value, "shard", [(0, 1), (1, 0)])


def run(kernel, ins, outs, scratch=(), flops=0, name=None):
    arrays, specs = [], []
    for item in ins:
        if isinstance(item, tuple):
            array, kind = item
            specs.append(pl.BlockSpec(memory_space=kind))
        else:
            array = item
            specs.append(pl.BlockSpec(memory_space=pltpu.VMEM))
        arrays.append(array)
    moved = sum(x.size * x.dtype.itemsize for x in arrays if x.size < 4_000_000)
    moved += sum(4 * x[0][0] * x[0][1] for x in outs)
    return pl.pallas_call(
        kernel,
        in_specs=specs,
        out_specs=[pl.BlockSpec(memory_space=pltpu.VMEM)] * len(outs),
        out_shape=[jax.ShapeDtypeStruct(shape, kind) for shape, kind in outs],
        scratch_shapes=list(scratch),
        compiler_params=pltpu.CompilerParams(vmem_limit_bytes=VMEM),
        cost_estimate=pl.CostEstimate(flops=flops, bytes_accessed=moved, transcendentals=0),
        name=name,
    )(*arrays)


def halves(s, own_ref, oth_ref, place, sems, first_sem, layer, columns=None):
    cols = slice(None) if columns is None else pl.ds(pl.multiple_of(columns, 128), FH)
    copies = []
    for k, (ref, half) in enumerate(((own_ref, s), (oth_ref, 1 - s))):
        rows = pl.ds(pl.multiple_of(half * HALF, 64), HALF)
        copies.append(
            pltpu.make_async_copy(
                ref.at[layer, :, cols], place.at[rows, :], sems.at[first_sem + k]
            )
        )
    return copies


def start(copies):
    for copy in copies:
        copy.start()


def wait(copies):
    for copy in copies:
        copy.wait()


def rms_parts(values):
    return lax.rsqrt(jnp.mean(values * values, axis=1, keepdims=True) + epsilon)


def rms_back(values, gain, grad):
    r = rms_parts(values)
    scaled = grad * gain
    back = r * scaled - values * (r * r * r * jnp.mean(values * scaled, axis=1, keepdims=True))
    return back, jnp.sum(grad * values * r, axis=0, keepdims=True)


def turn(values, cosine, sine):
    width = values.shape[1]
    times = width // 128
    lane = lax.broadcasted_iota(jnp.int32, values.shape, 1)
    partner = jnp.where(
        lane % HEAD < HEAD // 2,
        pltpu.roll(values, width - HEAD // 2, 1),
        pltpu.roll(values, HEAD // 2, 1),
    )
    cosine = jnp.concatenate([cosine] * times, axis=1)
    sine = jnp.concatenate([sine] * times, axis=1)
    return values * cosine + partner * sine


def take_half(value, mine):
    return jnp.where(mine == 0, value[:, :HALF], value[:, HALF:])


def qkv_kernel(
    layer, s_ref, x_ref, gain_ref, bias_ref, cos_ref, sin_ref, wo_ref, wx_ref,
    own_ref, oth_ref, q_ref, kv_ref, w, sems,
):
    s = s_ref[0]
    copies = halves(s, wo_ref, wx_ref, w, sems, 0, layer)
    start(copies)
    x = x_ref[...]
    normed = x * rms_parts(x) * gain_ref[...]
    own_ref[...] = take_half(normed, s).astype(BF)
    oth_ref[...] = take_half(normed, 1 - s).astype(BF)
    wait(copies)
    proj = jnp.dot(normed.astype(BF), w[...], preferred_element_type=F32) + bias_ref[...]
    turned = turn(proj[:, : D + 128], cos_ref[...], sin_ref[...]).astype(BF)
    q_ref[...] = turned[:, :D]
    kv_ref[:, :128] = turned[:, D:]
    kv_ref[:, 128:] = proj[:, D + 128 :].astype(BF)


def qkv(s, layer, x, gain, bias, cos, sin, w_own, w_oth):
    return run(
        functools.partial(qkv_kernel, layer),
        [(s, pltpu.SMEM), x, gain, bias, cos, sin, (w_own, pl.ANY), (w_oth, pl.ANY)],
        [((TOK, HALF), BF), ((TOK, HALF), BF), ((TOK, D), BF), ((TOK, 256), BF)],
        [pltpu.VMEM((D, QKV), BF), pltpu.SemaphoreType.DMA((2,))],
        flops=2 * TOK * D * QKV,
        name="qkv",
    )


def head(values, index):
    return values[:, index * HEAD : (index + 1) * HEAD]


def keys_values(kvo_ref, kvx_ref):
    kv = jnp.concatenate([kvo_ref[...], kvx_ref[...]], axis=0)
    return [head(kv, c) for c in range(KV_HEADS)], [head(kv, KV_HEADS + c) for c in range(KV_HEADS)]


def attn_kernel(
    layer, s_ref, q_ref, kvo_ref, kvx_ref, ok_ref, x_ref, gain_ref, wo_ref, wx_ref,
    own_ref, oth_ref, lse_ref, mid_ref, b_ref, w, mixed, sems,
):
    s = s_ref[0]
    copies = halves(s, wo_ref, wx_ref, w, sems, 0, layer)
    start(copies)
    keys, values = keys_values(kvo_ref, kvx_ref)
    allowed = ok_ref[...] > 0.0
    for h in range(HEADS):
        c = h * KV_HEADS // HEADS
        scores = contract_cols(head(q_ref, h), keys[c]) * HEAD**-0.5
        scores = jnp.where(allowed, scores, -1e30)
        top = jnp.max(scores, axis=1, keepdims=True)
        raised = jnp.exp(scores - top)
        total = jnp.sum(raised, axis=1, keepdims=True)
        probs = (raised / total).astype(BF)
        lse_ref[h] = top + jnp.log(total)
        mixed[:, h * HEAD : (h + 1) * HEAD] = jnp.dot(
            probs, values[c], preferred_element_type=F32
        )
    o = mixed[...]
    own_ref[...] = take_half(o, s).astype(BF)
    oth_ref[...] = take_half(o, 1 - s).astype(BF)
    wait(copies)
    middle = x_ref[...] + jnp.dot(o.astype(BF), w[...], preferred_element_type=F32)
    mid_ref[...] = middle
    b_ref[...] = (middle * rms_parts(middle) * gain_ref[...]).astype(BF)


def attn(s, layer, q, kv, kv_oth, allowed, x, gain, w_own, w_oth):
    return run(
        functools.partial(attn_kernel, layer),
        [(s, pltpu.SMEM), q, kv, kv_oth, allowed, x, gain, (w_own, pl.ANY), (w_oth, pl.ANY)],
        [
            ((TOK, HALF), BF),
            ((TOK, HALF), BF),
            ((HEADS, TOK, 1), F32),
            ((TOK, D), F32),
            ((TOK, D), BF),
        ],
        [pltpu.VMEM((D, D), BF), pltpu.VMEM((TOK, D), F32), pltpu.SemaphoreType.DMA((2,))],
        flops=2 * TOK * D * D + 4 * TOK * 256 * D,
        name="attn",
    )


def mlp_up_kernel(
    layer, s_ref, b_ref, bx_ref, gu_ref, gux_ref, wd_ref,
    own_ref, gate_ref, up_ref, m_ref, mine_ref, theirs_ref, wg, wu, wd, sems,
):
    s = s_ref[0]
    gates = halves(s, gu_ref, gux_ref, wg, sems, 0, layer, s * FH)
    ups = halves(s, gu_ref, gux_ref, wu, sems, 2, layer, FF + s * FH)
    down = [pltpu.make_async_copy(wd_ref.at[layer], wd, sems.at[4])]
    start(gates + ups + down)
    b = jnp.concatenate([b_ref[...], bx_ref[...]], axis=0)
    own_ref[...] = take_half(b.astype(F32), s).astype(BF)
    wait(gates)
    gate = jnp.dot(b, wg[...], preferred_element_type=F32)
    gate_ref[...] = gate.astype(BF)
    wait(ups)
    up = jnp.dot(b, wu[...], preferred_element_type=F32)
    up_ref[...] = up.astype(BF)
    m_ref[...] = (gate * jax.nn.sigmoid(gate) * up).astype(BF)
    wait(down)
    partial = jnp.dot(m_ref[...], wd[...], preferred_element_type=F32)
    mine_ref[...] = partial[:TOK]
    theirs_ref[...] = partial[TOK:]


WEIGHTS = (
    pltpu.VMEM((D, FH), BF),
    pltpu.VMEM((D, FH), BF),
    pltpu.VMEM((FH, D), BF),
    pltpu.SemaphoreType.DMA((5,)),
)


def mlp_up(s, layer, b, b_oth, w_own, w_oth, w_down):
    rows = 2 * TOK
    return run(
        functools.partial(mlp_up_kernel, layer),
        [(s, pltpu.SMEM), b, b_oth, (w_own, pl.ANY), (w_oth, pl.ANY), (w_down, pl.ANY)],
        [
            ((rows, HALF), BF),
            ((rows, FH), BF),
            ((rows, FH), BF),
            ((rows, FH), BF),
            ((TOK, D), F32),
            ((TOK, D), F32),
        ],
        WEIGHTS,
        flops=6 * rows * D * FH,
        name="mlp_up",
    )


def mlp_back_kernel(
    layer, s_ref, df_ref, dfx_ref, gate_ref, up_ref, gu_ref, gux_ref, wd_ref,
    dgu_ref, mine_ref, theirs_ref, wg, wu, wd, sems,
):
    s = s_ref[0]
    gates = halves(s, gu_ref, gux_ref, wg, sems, 0, layer, s * FH)
    ups = halves(s, gu_ref, gux_ref, wu, sems, 2, layer, FF + s * FH)
    down = [pltpu.make_async_copy(wd_ref.at[layer], wd, sems.at[4])]
    start(down + gates + ups)
    df = jnp.concatenate([df_ref[...], dfx_ref[...]], axis=0)
    wait(down)
    dm = contract_cols(df, wd[...])
    gate = gate_ref[...].astype(F32)
    sig = jax.nn.sigmoid(gate)
    dgu_ref[:, FH:] = (dm * gate * sig).astype(BF)
    dgu_ref[:, :FH] = (dm * up_ref[...].astype(F32) * (sig * (1.0 + gate * (1.0 - sig)))).astype(BF)
    wait(gates)
    db = contract_cols(dgu_ref[:, :FH], wg[...])
    wait(ups)
    db += contract_cols(dgu_ref[:, FH:], wu[...])
    mine_ref[...] = db[:TOK]
    theirs_ref[...] = db[TOK:]


def mlp_back(s, layer, df, df_oth, gate, up, w_own, w_oth, w_down):
    rows = 2 * TOK
    return run(
        functools.partial(mlp_back_kernel, layer),
        [(s, pltpu.SMEM), df, df_oth, gate, up]
        + [(w_own, pl.ANY), (w_oth, pl.ANY), (w_down, pl.ANY)],
        [((rows, 2 * FH), BF), ((TOK, D), F32), ((TOK, D), F32)],
        WEIGHTS,
        flops=6 * rows * D * FH,
        name="mlp_back",
    )


def attn_back_kernel(
    layer, s_ref, g_ref, db_ref, dbx_ref, mid_ref, gain_ref, q_ref, kvo_ref, kvx_ref, ok_ref,
    lse_ref, cos_ref, sin_ref, wo_ref, wx_ref,
    dh_ref, da_ref, dq_ref, mine_ref, theirs_ref, dgain_ref, w, dq, sems,
):
    s = s_ref[0]
    copies = halves(s, wo_ref, wx_ref, w, sems, 0, layer)
    start(copies)
    back, dgain_ref[...] = rms_back(mid_ref[...], gain_ref[...], db_ref[...] + dbx_ref[...])
    dh = g_ref[...] + back
    dh_ref[...] = dh
    da = dh.astype(BF)
    da_ref[...] = da
    wait(copies)
    do = contract_cols(da, w[...]).astype(BF)
    keys, values = keys_values(kvo_ref, kvx_ref)
    allowed = ok_ref[...] > 0.0
    dk = [jnp.zeros((2 * TOK, HEAD), F32) for c in range(KV_HEADS)]
    dv = [jnp.zeros((2 * TOK, HEAD), F32) for c in range(KV_HEADS)]
    for h in range(HEADS):
        c = h * KV_HEADS // HEADS
        q_h, do_h = head(q_ref, h), head(do, h)
        scores = contract_cols(q_h, keys[c]) * HEAD**-0.5
        probs = jnp.where(allowed, jnp.exp(scores - lse_ref[h]), 0.0)
        dp = contract_cols(do_h, values[c])
        dv[c] += contract_rows(probs.astype(BF), do_h)
        row_dot = jnp.sum(probs * dp, axis=1, keepdims=True)
        ds = (probs * (dp - row_dot)).astype(BF)
        dq[:, h * HEAD : (h + 1) * HEAD] = (
            jnp.dot(ds, keys[c], preferred_element_type=F32) * HEAD**-0.5
        )
        dk[c] += contract_rows(ds, q_h) * HEAD**-0.5
    dq_ref[...] = turn(dq[...], cos_ref[...], -sin_ref[...]).astype(BF)
    dkv = jnp.concatenate(dk + dv, axis=1)
    mine_ref[...] = dkv[:TOK]
    theirs_ref[...] = dkv[TOK:]


def attn_back(s, layer, g, db, db_oth, mid, gain, q, kv, kv_oth, ok, lse, cos, sin, w_own, w_oth):
    return run(
        functools.partial(attn_back_kernel, layer),
        [(s, pltpu.SMEM), g, db, db_oth, mid, gain, q, kv, kv_oth, ok, lse, cos, sin]
        + [(w_own, pl.ANY), (w_oth, pl.ANY)],
        [
            ((TOK, D), F32),
            ((TOK, D), BF),
            ((TOK, D), BF),
            ((TOK, 256), F32),
            ((TOK, 256), F32),
            ((1, D), F32),
        ],
        [pltpu.VMEM((D, D), BF), pltpu.VMEM((TOK, D), F32), pltpu.SemaphoreType.DMA((2,))],
        flops=2 * TOK * D * D + 10 * TOK * 256 * D,
        name="attn_back",
    )


def qkv_back_kernel(
    layer, s_ref, dq_ref, dkv_ref, dkvx_ref, dh_ref, x_ref, gain_ref, cos_ref, sin_ref, wo_ref, wx_ref,
    dproj_ref, g_ref, gb_ref, dgain_ref, w, sems,
):
    s = s_ref[0]
    copies = halves(s, wo_ref, wx_ref, w, sems, 0, layer)
    start(copies)
    dkv = dkv_ref[...] + dkvx_ref[...]
    dproj_ref[:, :D] = dq_ref[...]
    dproj_ref[:, D : D + 128] = turn(dkv[:, :128], cos_ref[...], -sin_ref[...]).astype(BF)
    dproj_ref[:, D + 128 :] = dkv[:, 128:].astype(BF)
    wait(copies)
    da = contract_cols(dproj_ref[...], w[...])
    back, dgain_ref[...] = rms_back(x_ref[...], gain_ref[...], da)
    g = dh_ref[...] + back
    g_ref[...] = g
    gb_ref[...] = g.astype(BF)


def qkv_back(s, layer, dq, dkv, dkv_oth, dh, x, gain, cos, sin, w_own, w_oth):
    return run(
        functools.partial(qkv_back_kernel, layer),
        [(s, pltpu.SMEM), dq, dkv, dkv_oth, dh, x, gain, cos, sin]
        + [(w_own, pl.ANY), (w_oth, pl.ANY)],
        [((TOK, QKV), BF), ((TOK, D), F32), ((TOK, D), BF), ((1, D), F32)],
        [pltpu.VMEM((D, QKV), BF), pltpu.SemaphoreType.DMA((2,))],
        flops=2 * TOK * D * QKV,
        name="qkv_back",
    )


def whole(shape):
    return pl.BlockSpec(shape, lambda i, s: (0,) * len(shape))


def store_columns(out_ref, at, value):
    high = value.shape[0] // TILE
    for c in range(value.shape[1] // 128):
        piece = value[:, c * 128 : (c + 1) * 128].reshape(high, TILE, 128)
        out_ref[at + c * high : at + (c + 1) * high] = piece.astype(BF)


def grad_gu_kernel(s_ref, b_ref, own_ref, oth_ref, out_ref):
    mine = lax.rem(pl.program_id(0), 2) == s_ref[0]

    @pl.when(mine)
    def _():
        store_columns(out_ref, 0, contract_rows(b_ref[...], own_ref[...]))

    @pl.when(jnp.logical_not(mine))
    def _():
        turned = jnp.concatenate([b_ref[TOK:], b_ref[:TOK]], axis=0)
        store_columns(out_ref, 0, contract_rows(turned, oth_ref[...]))


def grad_gu(s, b, dgu_own, dgu_oth):
    rows = dgu_own.shape[0]
    return pl.pallas_call(
        grad_gu_kernel,
        grid_spec=pltpu.PrefetchScalarGridSpec(
            num_scalar_prefetch=1,
            grid=(4,),
            in_specs=[
                whole((rows, HALF)),
                pl.BlockSpec((rows, FH), lambda i, s: (0, i // 2)),
                pl.BlockSpec((rows, FH), lambda i, s: (0, i // 2)),
            ],
            out_specs=pl.BlockSpec((GU_TILES, TILE, 128), lambda i, s: (i, 0, 0)),
        ),
        out_shape=jax.ShapeDtypeStruct((TILES, TILE, 128), BF),
        compiler_params=pltpu.CompilerParams(vmem_limit_bytes=VMEM),
        cost_estimate=pl.CostEstimate(
            flops=4 * rows * HALF * FF, bytes_accessed=14_000_000, transcendentals=0
        ),
        name="grad_gu",
    )(s, b, dgu_own, dgu_oth)


def grad_down_kernel(m_ref, df_ref, dfx_ref, old_ref, out_ref):
    df = jnp.concatenate([df_ref[...], dfx_ref[...]], axis=0)
    store_columns(out_ref, 0, contract_rows(m_ref[...], df))


def grad_rest_kernel(
    a_ref, ax_ref, dp_ref, dpx_ref, o_ref, ox_ref, da_ref, dax_ref, vec_ref, old_ref, out_ref
):
    a = jnp.concatenate([a_ref[...], ax_ref[...]], axis=0)
    dp = jnp.concatenate([dp_ref[...], dpx_ref[...]], axis=0)
    store_columns(out_ref, 0, contract_rows(a, dp))
    o = jnp.concatenate([o_ref[...], ox_ref[...]], axis=0)
    da = jnp.concatenate([da_ref[...], dax_ref[...]], axis=0)
    store_columns(out_ref, 252, contract_rows(o, da))
    out_ref[448:] = vec_ref[...]


def fill(kernel, ins, packed, tiles, index, flops, name):
    return pl.pallas_call(
        kernel,
        grid=(1,),
        in_specs=[pl.BlockSpec(x.shape, lambda i, n=x.ndim: (0,) * n) for x in ins]
        + [pl.BlockSpec(memory_space=pl.ANY)],
        out_specs=pl.BlockSpec((tiles, TILE, 128), lambda i: (index, 0, 0)),
        out_shape=jax.ShapeDtypeStruct(packed.shape, BF),
        input_output_aliases={len(ins): 0},
        compiler_params=pltpu.CompilerParams(vmem_limit_bytes=VMEM),
        cost_estimate=pl.CostEstimate(
            flops=flops, bytes_accessed=2 * tiles * TILE * 128, transcendentals=0
        ),
        name=name,
    )(*ins, packed)


def chunk_copies(table_ref, from_ref, place, sem, first, count):
    def one(n, carry):
        tiles = pl.ds(n * CHUNK, CHUNK)
        pltpu.make_async_copy(from_ref.at[table_ref[n]], place.at[tiles], sem).start()
        return carry

    lax.fori_loop(first, first + count, one, 0)


def unpack_kernel(layer, olds, table_ref, from_ref, *refs):
    out_q, out_o, out_gu, out_d, vec_ref, place, stage_gu, stage_d, stage_q, stage_o, sems, out_sems = refs[olds:]
    for j in range(4):
        chunk_copies(table_ref, from_ref, place, sems.at[j], 28 * j, 28)
    chunk_copies(table_ref, from_ref, place, sems.at[4], 112, 56)
    chunk_copies(table_ref, from_ref, place, sems.at[5], 168, 24)

    def arrived(first, tiles, sem):
        part = place.at[first : first + tiles]
        pltpu.make_async_copy(part, part, sem).wait()

    def spread(stage, first):
        rows = stage.shape[0]
        high = rows // TILE
        for c in range(stage.shape[1] // 128):
            piece = place[first + c * high : first + (c + 1) * high]
            stage[:, c * 128 : (c + 1) * 128] = piece.astype(F32).reshape(rows, 128)

    sent = []
    for j in range(4):
        arrived(j * GU_TILES, GU_TILES, sems.at[j])
        if j >= 2:
            sent[j - 2].wait()
        spread(stage_gu.at[j % 2], j * GU_TILES)
        copy = pltpu.make_async_copy(
            stage_gu.at[j % 2], out_gu.at[layer, :, j * FH : (j + 1) * FH], out_sems.at[j]
        )
        copy.start()
        sent.append(copy)
    first = 4 * GU_TILES
    arrived(first, DOWN_TILES, sems.at[4])
    spread(stage_d, first)
    sent.append(pltpu.make_async_copy(stage_d, out_d.at[layer], out_sems.at[4]))
    sent[4].start()
    first += DOWN_TILES
    arrived(first, REST_TILES, sems.at[5])
    spread(stage_q, first)
    sent.append(pltpu.make_async_copy(stage_q, out_q.at[layer], out_sems.at[5]))
    sent[5].start()
    spread(stage_o, first + 252)
    sent.append(pltpu.make_async_copy(stage_o, out_o.at[layer], out_sems.at[6]))
    sent[6].start()
    vec_ref[...] = place[first + 448 : first + 456].astype(F32)
    for copy in sent[2:]:
        copy.wait()


def unpack(table, gathered, layer, olds):
    shapes = [(2, HALF, QKV), (2, HALF, D), (2, HALF, 2 * FF), (2, FH, D)]
    return pl.pallas_call(
        functools.partial(unpack_kernel, layer, len(olds)),
        in_specs=[pl.BlockSpec(memory_space=pltpu.SMEM)]
        + [pl.BlockSpec(memory_space=pl.ANY)] * (1 + len(olds)),
        out_specs=[pl.BlockSpec(memory_space=pl.ANY)] * 4 + [pl.BlockSpec(memory_space=pltpu.VMEM)],
        out_shape=[jax.ShapeDtypeStruct(shape, F32) for shape in shapes]
        + [jax.ShapeDtypeStruct((8, TILE, 128), F32)],
        input_output_aliases={2 + i: i for i in range(len(olds))},
        scratch_shapes=[
            pltpu.VMEM((TILES, TILE, 128), BF),
            pltpu.VMEM((2, HALF, FH), F32),
            pltpu.VMEM((FH, D), F32),
            pltpu.VMEM((HALF, QKV), F32),
            pltpu.VMEM((HALF, D), F32),
            pltpu.SemaphoreType.DMA((6,)),
            pltpu.SemaphoreType.DMA((7,)),
        ],
        compiler_params=pltpu.CompilerParams(vmem_limit_bytes=VMEM),
        cost_estimate=pl.CostEstimate(flops=0, bytes_accessed=45_000_000, transcendentals=0),
        name="unpack",
    )(table, gathered, *olds)


ORDERS = (("x", "y", "z"), ("y", "z", "x"), ("z", "x", "y"))
STRIDE = {"x": 1, "y": 4, "z": 16}


def pairing(axis, stage):
    pairs = []
    for rep in range(64):
        at = rep // STRIDE[axis] % 4
        for core in range(2):
            to = at ^ 1 if stage == core else 3 - at
            pairs.append((rep * 2 + core, (rep + (to - at) * STRIDE[axis]) * 2 + core))
    return pairs


def kept_half(rep, core, axis, stage):
    at = rep // STRIDE[axis] % 4
    if core == 0:
        return ((at + 1) // 2) % 2 if stage == 0 else at // 2
    return at // 2 if stage == 0 else at % 2


def all_steps(flow):
    return [(axis, stage) for axis in ORDERS[flow] for stage in (0, 1)]


def chunk_table(core):
    table = [0] * 192
    for rep in range(64):
        for flow in range(3):
            index = 0
            for axis, stage in all_steps(flow):
                index = index * 2 + kept_half(rep, core, axis, stage)
            table[flow * 64 + index] = rep * 3 + flow
    return jnp.array(table, jnp.int32)


def scatter_sum(packed):
    count = TILES // 3
    rep = lax.axis_index("rep")
    first = lax.axis_index("shard") == 0
    kept = [packed] * 3
    got = [None] * 3
    for step in range(7):
        half = count >> (step + 1)
        for flow in range(3):

            def part(start, size):
                if step == 0:
                    return lax.dynamic_slice_in_dim(packed, flow * count + start, size, 0)
                a = lax.dynamic_slice_in_dim(kept[flow], start, size, 0).astype(F32)
                b = lax.dynamic_slice_in_dim(got[flow], start, size, 0).astype(F32)
                return (a + b).astype(BF)

            if step == 6:
                kept[flow] = part(0, CHUNK)
                continue
            axis, stage = all_steps(flow)[step]
            keep = jnp.where(first, kept_half(rep, 0, axis, stage), kept_half(rep, 1, axis, stage))
            sent = part((1 - keep) * half, half)
            mine = part(keep * half, half)
            got[flow] = lax.ppermute(sent, ("rep", "shard"), pairing(axis, stage))
            kept[flow] = mine
    return jnp.concatenate(kept)


def gather_sum(chunks):
    gathered = lax.all_gather(chunks, "rep", axis=0, tiled=True)
    return gathered.reshape(192, CHUNK, TILE, 128)


def body(
    hidden_in,
    seq_lengths,
    block_owner,
    norm_attn,
    w_qkv,
    b_qkv,
    w_out,
    norm_mlp,
    w_gate_up,
    w_down,
    grad_out,
):
    layer_count = 2
    me = lax.axis_index("shard")
    first = me == 0
    s_arr = me.astype(jnp.int32).reshape(1)

    def own_half(value, size):
        return jnp.where(first, value[..., :size], value[..., size:])

    def other_half(value, size):
        return jnp.where(first, value[..., size:], value[..., :size])

    def join(mine, theirs):
        return jnp.where(
            first,
            jnp.concatenate([mine, theirs], axis=1),
            jnp.concatenate([theirs, mine], axis=1),
        ).astype(F32)

    small_own = jnp.concatenate([norm_attn, b_qkv, norm_mlp], axis=1)
    small_oth = swap(small_own)
    wq_oth = swap(w_qkv)
    wo_oth = swap(w_out)
    gu_oth = swap(w_gate_up)
    out_grad = grad_out.astype(BF)
    gains_attn = join(small_own[:, :HALF], small_oth[:, :HALF])
    biases = join(small_own[:, HALF:-HALF], small_oth[:, HALF:-HALF])
    gains_mlp = join(small_own[:, -HALF:], small_oth[:, -HALF:])

    lengths = seq_lengths[0]
    owner_row = block_owner[0]
    offsets = jnp.arange(TOK, dtype=jnp.int32)
    my_stream = owner_row[me] * TOK + offsets
    key_stream = jnp.concatenate([my_stream, owner_row[1 - me] * TOK + offsets])
    key_docs, key_pos = doc_position(key_stream, lengths)
    my_docs, positions = doc_position(my_stream, lengths)
    allowed = (my_docs[:, None] == key_docs[None, :]) & (key_stream[None, :] <= my_stream[:, None])
    allowed = allowed.astype(F32)
    cosine, sine_part = angles(positions, HEAD)
    cos = jnp.concatenate([cosine] * 4, axis=1)
    sin = jnp.concatenate([-sine_part, sine_part] * 2, axis=1)

    residual = hidden_in.astype(F32)
    kept_state = []
    for layer in range(layer_count):
        gain_a = gains_attn[layer : layer + 1]
        gain_m = gains_mlp[layer : layer + 1]
        a_own, a_send, q, kv = qkv(
            s_arr, layer, residual, gain_a, biases[layer : layer + 1], cos, sin, w_qkv, wq_oth
        )
        kv_oth = swap(kv)
        o_own, o_send, lse, middle, b = attn(
            s_arr, layer, q, kv, kv_oth, allowed, residual, gain_m, w_out, wo_oth
        )
        b_oth = swap(b)
        a_oth = swap(a_send)
        o_oth = swap(o_send)
        b_own, gate, up, hidden, mine, theirs = mlp_up(
            s_arr, layer, b, b_oth, w_gate_up, gu_oth, w_down
        )
        a_pair = (a_own, a_oth)
        o_pair = (o_own, o_oth)
        kept_state.append(
            (residual, a_pair, q, kv, kv_oth, lse, o_pair, middle, b_own, gate, up, hidden, gain_a, gain_m)
        )
        residual = middle + mine + swap(theirs)

    grad_resid = grad_out
    for layer in reversed(range(layer_count)):
        resid_in, a_pair, q, kv, kv_oth, lse, o_pair, middle, b_own, gate, up, hidden, gain_a, gain_m = (
            kept_state[layer]
        )
        out_oth = swap(out_grad)
        dgu, db, db_send = mlp_back(
            s_arr, layer, out_grad, out_oth, gate, up, w_gate_up, gu_oth, w_down
        )
        db_oth = swap(db_send)
        dgu_oth = swap(dgu)
        down_grad = (out_grad, out_oth)
        dh, da, dq, dkv, dkv_send, gain_m_grad = attn_back(
            s_arr, layer, grad_resid, db, db_oth, middle, gain_m, q, kv, kv_oth, allowed, lse,
            cos, sin, w_out, wo_oth,
        )
        dkv_oth = swap(dkv_send)
        da_oth = swap(da)
        dproj, grad_resid, out_grad, gain_a_grad = qkv_back(
            s_arr, layer, dq, dkv, dkv_oth, dh, resid_in, gain_a, cos, sin, w_qkv, wq_oth
        )
        dproj_oth = swap(dproj)
        grad_bias = jnp.sum(dproj.astype(F32), axis=0) + jnp.sum(dproj_oth.astype(F32), axis=0)
        gains = jnp.concatenate([gain_a_grad, gain_m_grad], axis=0)
        gains = own_half(gains, HALF) + swap(other_half(gains, HALF))
        vectors = jnp.concatenate([gains[0], gains[1], own_half(grad_bias, QKV // 2)])
        vectors = jnp.pad(vectors, (0, 8 * TILE * 128 - vectors.shape[0])).astype(BF)
        packed = grad_gu(s_arr, b_own, dgu, dgu_oth)
        packed = fill(
            grad_down_kernel, (hidden,) + down_grad, packed, DOWN_TILES, 2, 4 * TOK * FH * D, "grad_down"
        )
        packed = fill(
            grad_rest_kernel,
            a_pair + (dproj, dproj_oth) + o_pair + (da, da_oth) + (vectors.reshape(8, TILE, 128),),
            packed,
            REST_TILES,
            7,
            4 * TOK * HALF * (QKV + D),
            "grad_rest",
        )
        if layer == 1:
            grad_resid, out_grad, packed = lax.optimization_barrier((grad_resid, out_grad, packed))
            upper_sum = lax.psum(packed, "rep").reshape(192, CHUNK, TILE, 128)
        else:
            lower_chunks = scatter_sum(packed)
    table = jnp.where(first, chunk_table(0), chunk_table(1))
    *grads, upper = unpack(jnp.arange(192, dtype=jnp.int32), upper_sum, 1, [])
    *grads, lower = unpack(table, gather_sum(lower_chunks), 0, grads)
    vectors = jnp.stack([lower.reshape(-1)[:1472], upper.reshape(-1)[:1472]])
    return (
        residual.astype(BF),
        grad_resid,
        vectors[:, :HALF],
        grads[0],
        vectors[:, 2 * HALF :],
        grads[1],
        vectors[:, HALF : 2 * HALF],
        grads[2],
        grads[3],
    )


def solution(mesh):
    placed = (
        P(("rep", "shard"), None),
        P("rep", None),
        P("rep", None),
        P(None, "shard"),
        P(None, "shard", None),
        P(None, "shard"),
        P(None, "shard", None),
        P(None, "shard"),
        P(None, "shard", None),
        P(None, "shard", None),
        P(("rep", "shard"), None),
    )
    return jax.shard_map(
        body,
        mesh=mesh,
        in_specs=placed,
        out_specs=(
            P(("rep", "shard"), None),
            P(("rep", "shard"), None),
            P(None, "shard"),
            P(None, "shard", None),
            P(None, "shard"),
            P(None, "shard", None),
            P(None, "shard"),
            P(None, "shard", None),
            P(None, "shard", None),
        ),
        check_vma=False,
    )
```
